32 devices in a mesh: req: 8 (over y, x, core), tp: 4 (over z).
Axes of the slice: x: 2, y: 2, z: 4, core: 2. Of those that a mesh axis runs over, the one named last changes fastest.
Arguments:
- tokens: bfloat16 [8, 768, 2048], P('req', None, 'tp'), may hold values from -6 to 6
- q_weight: bfloat16 [2048, 2048], P(None, 'tp'), may hold values from -0.125 to 0.125
- k_weight: bfloat16 [2048, 2048], P(None, 'tp'), may hold values from -0.125 to 0.125
- v_weight: bfloat16 [2048, 2048], P(None, 'tp'), may hold values from -0.125 to 0.125
- o_weight: bfloat16 [2048, 2048], P('tp'), may hold values from -0.125 to 0.125
- q_gain: bfloat16 [2048], P('tp'), may hold values from 0.099609375 to 1.8984375
- k_gain: bfloat16 [2048], P('tp'), may hold values from 0.099609375 to 1.8984375
- post_gain: bfloat16 [2048], P('tp'), may hold values from 0.099609375 to 1.8984375
- key_pool: bfloat16 [256, 128, 2048], P('req', None, 'tp'), may hold values from -400 to 400
- value_pool: bfloat16 [256, 128, 2048], P('req', None, 'tp'), may hold values from -6 to 6
- cache_len: int32 [8], replicated, may hold values from 1 to 4096, as said below
- page_table: int32 [8, 32], replicated, may hold values from -1 to 255, as said below
Outputs:
- mixed: bfloat16 [8, 768, 2048], P('req', None, 'tp')
- new_keys: bfloat16 [8, 768, 2048], P('req', None, 'tp')
- new_values: bfloat16 [8, 768, 2048], P('req', None, 'tp')
The draws below stay inside these ranges and needn't reach their ends.
Inputs may be any that keep to these rules, and one draw needn't show every extreme that they name: `cache_len`: on some index of req the one request hold 4096 cached tokens. `page_table`: entry p of request r is a pool page (index d * 32 + local page of index d of req) for p < ceil(cache_len[r] / 128) and -1 otherwise; no pool page is named twice; the pages named by the requests of one index of req lie at most 4 on any one index of req, and some pair of indices reaches 4.
All inputs are finite; a program needn't handle non-finite values.
Results may differ from the reference program's by a relative error of at most 0.013.
Values may be sent and summed in bfloat16 or wider, within the bound.
A program may use at most 128 MiB of HBM per device.

```python
import jax
import jax.numpy as jnp
from jax import lax

D = 2048
HEADS = 16
HEAD_DIM = 128
BLOCK = 768
REQ_DEV = 1
PAGE = 128
MAXLEN = 4096
MAXPAGES = 32
REQS = 8
POOLS = 256
N_TP = 4


def request_lengths(key):
    owners = REQS // REQ_DEV
    lengths = jax.random.randint(jax.random.fold_in(key, 11), (REQS,), 1, MAXLEN + 1)
    chosen = jax.random.randint(jax.random.fold_in(key, 14), (), 0, owners)
    owner_of = jnp.arange(REQS) // REQ_DEV
    return jnp.where(owner_of == chosen, MAXLEN, lengths).astype(jnp.int32)


def draw_cache_len(key, part):
    return request_lengths(key)


def draw_page_table(key, part):
    lengths = request_lengths(key)
    owners = REQS // REQ_DEV
    per_owner = REQ_DEV * MAXPAGES
    pool_dev = per_owner
    pair_cap = pool_dev // owners
    page_count = (lengths + PAGE - 1) // PAGE
    valid = (jnp.arange(MAXPAGES)[None, :] < page_count[:, None]).reshape(owners, per_owner)
    offsets = jax.random.randint(jax.random.fold_in(key, 12), (owners, 1), 0, owners)
    source = (offsets + jnp.arange(per_owner)[None, :]) % owners
    order = jnp.arange(per_owner)
    same = (source[:, :, None] == source[:, None, :]) & valid[:, None, :] & (order[None, :, None] > order[None, None, :])
    rank = jnp.sum(same.astype(jnp.int32), -1)
    shuffles = jax.vmap(lambda sub_key: jax.random.permutation(sub_key, pool_dev))(jax.random.split(jax.random.fold_in(key, 13), owners))
    owner_ids = jnp.arange(owners)[:, None]
    slot_ids = jnp.clip(owner_ids * pair_cap + rank, 0, pool_dev - 1)
    local = shuffles[source, slot_ids]
    table = jnp.where(valid, source * pool_dev + local, -1)
    return table.reshape(REQS, MAXPAGES).astype(jnp.int32)


def draw_key_pool(key, part):
    base = jax.random.normal(jax.random.fold_in(key, 21), (POOLS, PAGE, HEADS * HEAD_DIM), jnp.float32)
    base = jnp.clip(base, -6.0, 6.0)
    return base.astype(jnp.bfloat16)


def levels(stream_key, extent, pieces, least, high):
    def one(axis_at, parts):
        steps = jax.random.uniform(jax.random.fold_in(jax.random.fold_in(stream_key, 6), axis_at), (parts,), jnp.float32, least / len(pieces), high / len(pieces))
        return jnp.repeat(jnp.exp(steps), extent[axis_at] // parts).reshape((-1,) + (1,) * (len(extent) - axis_at - 1))

    level = one(*pieces[0])
    for cut in pieces[1:]:
        level = level * one(*cut)
    return level


def noise(rng, extent, scale, reach, cuts=(), held_as=jnp.bfloat16):
    entries = jax.random.normal(rng, extent, jnp.float32) * scale
    if len(cuts) > 0:
        entries = levels(rng, extent, cuts, -0.22, 0.18) * entries
    return jnp.clip(entries, min=-reach, max=reach).astype(held_as)


def setup_inputs(seed: int = 0) -> dict:
    key_list = jax.random.split(jax.random.key(seed), 13)
    tokens = noise(key_list[0], (REQS, BLOCK, D), 1.0, 6.0, ((0, 8), (2, 4)))
    q_weight = noise(key_list[1], (D, HEADS * HEAD_DIM), D ** -0.5, 0.125, ((1, 4),))
    k_weight = noise(key_list[2], (D, HEADS * HEAD_DIM), D ** -0.5, 0.125, ((1, 4),))
    v_weight = noise(key_list[3], (D, HEADS * HEAD_DIM), D ** -0.5, 0.125, ((1, 4),))
    o_weight = noise(key_list[4], (HEADS * HEAD_DIM, D), (HEADS * HEAD_DIM) ** -0.5, 0.125, ((0, 4),))
    q_gain = jnp.clip(1.0 + 0.18 * jax.random.normal(key_list[5], (HEADS * HEAD_DIM,), jnp.float32), 0.099609375, 1.8984375).astype(jnp.bfloat16)
    k_gain = jnp.clip(1.0 + 0.18 * jax.random.normal(key_list[6], (HEADS * HEAD_DIM,), jnp.float32), 0.099609375, 1.8984375).astype(jnp.bfloat16)
    post_gain = jnp.clip(1.0 + 0.18 * jax.random.normal(key_list[7], (D,), jnp.float32), 0.099609375, 1.8984375).astype(jnp.bfloat16)
    key_pool = draw_key_pool(jax.random.fold_in(key_list[12], 71), 0)
    value_pool = noise(key_list[9], (POOLS, PAGE, HEADS * HEAD_DIM), 1.0, 6.0, ((0, 8), (2, 4)))
    cache_len = draw_cache_len(jax.random.fold_in(key_list[12], 71), 0)
    page_table = draw_page_table(jax.random.fold_in(key_list[12], 71), 0)
    return {"tokens": tokens, "q_weight": q_weight, "k_weight": k_weight, "v_weight": v_weight, "o_weight": o_weight, "q_gain": q_gain, "k_gain": k_gain, "post_gain": post_gain, "key_pool": key_pool, "value_pool": value_pool, "cache_len": cache_len, "page_table": page_table}


EPSILON = 1e-06
ROPE_BASE = 500000.0

def rotate(values, positions):
    half_dim = values.shape[-1] // 2
    freqs = jnp.power(jnp.float32(ROPE_BASE), -jnp.arange(half_dim, dtype=jnp.float32) * 2.0 / values.shape[-1])
    angles = positions[..., None] * freqs
    cosine = jnp.cos(angles)[..., None, :]
    sine_part = jnp.sin(angles)[..., None, :]
    first_half = values[..., :half_dim]
    second_half = values[..., half_dim:]
    return jnp.concatenate([first_half * cosine - second_half * sine_part, second_half * cosine + first_half * sine_part], -1)

def attend(query, cache_k, cache_v, fresh_k, fresh_v, lengths):
    scale = query.shape[-1] ** (-0.5)
    block_len = query.shape[1]
    cache_span = cache_k.shape[1]
    query_f = query.astype(jnp.float32)
    cache_scores = jnp.einsum('rqhd,rkhd->rhqk', query_f, cache_k.astype(jnp.float32)) * scale
    fresh_scores = jnp.einsum('rqhd,rkhd->rhqk', query_f, fresh_k.astype(jnp.float32)) * scale
    cache_mask = (jnp.arange(cache_span)[None, :] < lengths[:, None])[:, None, None, :]
    causal = (jnp.arange(block_len)[:, None] >= jnp.arange(block_len)[None, :])[None, None]
    scores = jnp.concatenate([jnp.where(cache_mask, cache_scores, -1e+30), jnp.where(causal, fresh_scores, -1e+30)], -1)
    peak = lax.optimization_barrier(jnp.max(scores, -1, keepdims=True))
    raised = jnp.exp(scores - peak)
    weights = (raised / lax.optimization_barrier(jnp.sum(raised, -1, keepdims=True))).astype(jnp.bfloat16)
    weights_f = weights.astype(jnp.float32)
    result = jnp.einsum('rhqk,rkhd->rqhd', weights_f[..., :cache_span], cache_v.astype(jnp.float32))
    result = result + jnp.einsum('rhqk,rkhd->rqhd', weights_f[..., cache_span:], fresh_v.astype(jnp.float32))
    return result.astype(jnp.bfloat16).reshape(query.shape[0], block_len, -1)

def reference(tokens, q_weight, k_weight, v_weight, o_weight, q_gain, k_gain, post_gain, key_pool, value_pool, cache_len, page_table):
    row_count = REQS * BLOCK
    columns = HEADS * HEAD_DIM
    flat = tokens.reshape(row_count, D)
    q_proj = jnp.dot(flat, q_weight, preferred_element_type=jnp.float32)
    k_proj = jnp.dot(flat, k_weight, preferred_element_type=jnp.float32)
    new_values = jnp.dot(flat, v_weight, preferred_element_type=jnp.float32).astype(jnp.bfloat16)
    q_normed = q_proj * lax.rsqrt(lax.optimization_barrier(jnp.mean(q_proj * q_proj, 1)) + EPSILON)[:, None] * q_gain.astype(jnp.float32)
    k_normed = k_proj * lax.rsqrt(lax.optimization_barrier(jnp.mean(k_proj * k_proj, 1)) + EPSILON)[:, None] * k_gain.astype(jnp.float32)
    positions = (cache_len[:, None] + jnp.arange(BLOCK, dtype=jnp.int32)[None, :]).astype(jnp.float32)
    query = rotate(q_normed.reshape(REQS, BLOCK, HEADS, HEAD_DIM), positions).astype(jnp.bfloat16)
    new_keys = rotate(k_normed.reshape(REQS, BLOCK, HEADS, HEAD_DIM), positions).astype(jnp.bfloat16)
    fresh_values = new_values.reshape(REQS, BLOCK, HEADS, HEAD_DIM)

    def one_request(items):
        query_r, key_r, value_r, length_r, table_r = items
        chosen = jnp.maximum(table_r, 0).astype(jnp.int32)
        cache_k = key_pool[chosen].reshape(MAXLEN, HEADS, HEAD_DIM)
        cache_v = value_pool[chosen].reshape(MAXLEN, HEADS, HEAD_DIM)
        return attend(query_r[None], cache_k[None], cache_v[None], key_r[None], value_r[None], length_r[None])[0]
    attended = lax.map(one_request, (query, new_keys, fresh_values, cache_len, page_table))
    attended = attended.reshape(row_count, columns)
    group = columns // N_TP
    projected = jnp.zeros((row_count, D), jnp.float32)
    for index in range(N_TP):
        part = jnp.dot(attended[:, index * group:(index + 1) * group], o_weight[index * group:(index + 1) * group], preferred_element_type=jnp.float32)
        rounded = lax.optimization_barrier(part.astype(jnp.bfloat16))
        projected = projected + rounded.astype(jnp.float32)
    normed = projected * lax.rsqrt(lax.optimization_barrier(jnp.mean(projected * projected, 1)) + EPSILON)[:, None]
    mixed = (flat.astype(jnp.float32) + normed * post_gain.astype(jnp.float32)).astype(jnp.bfloat16)
    return (mixed.reshape(REQS, BLOCK, D), new_keys.reshape(REQS, BLOCK, columns), new_values.reshape(REQS, BLOCK, columns))
```

```python
import functools

import jax
import jax.numpy as jnp
from jax import lax
from jax.experimental import pallas as pl
from jax.experimental.pallas import tpu as pltpu
from jax.sharding import PartitionSpec as P

HEAD_DIM = 128
EPSILON = 1e-06
ROPE_BASE = 500000.0
ROWS = 256
SLOTS = 8


def head_groups(heads):
    return (heads - 2, 1, 1) if heads > 2 else (1,) * heads


def page_slots(page_table, pool_dev):
    valid = page_table >= 0
    source = jnp.where(valid, page_table // pool_dev, -1)
    local = jnp.where(valid, page_table % pool_dev, 0)
    order = jnp.arange(page_table.shape[1])
    same = (
        (source[:, :, None] == source[:, None, :])
        & valid[:, None, :]
        & (order[None, :, None] > order[None, None, :])
    )
    rank = jnp.sum(same.astype(jnp.int32), -1)
    return (source, rank, valid, local)


def collect_kernel(first, width, chosen, key_pool, value_pool, out, sem):
    columns = pl.ds(first, width)

    def copies(slot):
        page = chosen[slot]
        return (
            pltpu.make_async_copy(key_pool.at[page, :, columns], out.at[slot, 0], sem),
            pltpu.make_async_copy(value_pool.at[page, :, columns], out.at[slot, 1], sem),
        )

    @pl.loop(0, out.shape[0])
    def _(slot):
        for copy in copies(slot):
            copy.start()

    pltpu.make_async_copy(out, out, sem).wait()


def collect(first, width, chosen, key_pool, value_pool):
    slots = chosen.shape[0]
    page_len = key_pool.shape[1]
    return pl.pallas_call(
        functools.partial(collect_kernel, first, width),
        out_shape=jax.ShapeDtypeStruct((slots, 2, page_len, width), key_pool.dtype),
        in_specs=[
            pl.BlockSpec(memory_space=pltpu.SMEM),
            pl.BlockSpec(memory_space=pl.ANY),
            pl.BlockSpec(memory_space=pl.ANY),
        ],
        out_specs=pl.BlockSpec(memory_space=pl.ANY),
        scratch_shapes=[pltpu.SemaphoreType.DMA],
        name="collect",
    )(chosen, key_pool, value_pool)


def norm_rope_kernel(q, k, q_scale, k_scale, q_gain, k_gain, cosine, sine, q_out, k_out):
    cos, sin = cosine[...], sine[...]
    for values, scale, gain, out in ((q, q_scale, q_gain, q_out), (k, k_scale, k_gain, k_out)):
        for head in range(values.shape[1] // HEAD_DIM):
            part = pl.ds(head * HEAD_DIM, HEAD_DIM)
            x = values[:, part] * scale[...] * gain[:, part]
            out[:, part] = (x * cos + pltpu.roll(x, HEAD_DIM // 2, 1) * sin).astype(out.dtype)


def norm_rope(q, k, q_scale, k_scale, q_gain, k_gain, cosine, sine):
    rows, columns = q.shape
    block = ROWS
    wide = pl.BlockSpec((block, columns), lambda i: (i, 0))
    thin = pl.BlockSpec((block, 1), lambda i: (i, 0))
    flat = pl.BlockSpec((1, columns), lambda i: (0, 0))
    half = pl.BlockSpec((block, HEAD_DIM), lambda i: (i, 0))
    shape = jax.ShapeDtypeStruct((rows, columns), jnp.bfloat16)
    return pl.pallas_call(
        norm_rope_kernel,
        grid=(rows // block,),
        out_shape=(shape, shape),
        in_specs=[wide, wide, thin, thin, flat, flat, half, half],
        out_specs=(wide, wide),
        compiler_params=pltpu.CompilerParams(vmem_limit_bytes=32 * 2**20),
        name="norm_rope",
    )(q, k, q_scale, k_scale, q_gain, k_gain, cosine, sine)


NT = (((1,), (1,)), ((), ()))


def attend_kernel(factor, chunks, state, q, kv, fresh_k, fresh_v, bias, out, m_ref, l_ref, acc_ref):
    rows = q.shape[0]
    tiles = rows // ROWS
    span = SLOTS * kv.shape[3]

    def update(part, scores, values):
        m_old = m_ref[part, :1]
        m_new = jnp.maximum(m_old, jnp.max(scores, 1, keepdims=True))
        alpha = jnp.exp2(m_old * factor - m_new * factor)
        raised = jnp.exp2(scores * factor - m_new * factor)
        total = l_ref[part, :1] * alpha + jnp.sum(raised, 1, keepdims=True)
        acc_ref[part] = acc_ref[part] * alpha + jnp.dot(
            raised.astype(jnp.bfloat16), values, preferred_element_type=jnp.float32
        )
        m_ref[part] = jnp.broadcast_to(m_new, (ROWS, HEAD_DIM))
        l_ref[part] = jnp.broadcast_to(total, (ROWS, HEAD_DIM))

    for tile in range(tiles):
        part = pl.ds(tile * ROWS, ROWS)
        reach = (tile + 1) * ROWS
        scores = lax.dot_general(
            q[part], fresh_k[:reach], NT, preferred_element_type=jnp.float32
        )
        row = lax.broadcasted_iota(jnp.int32, scores.shape, 0) + tile * ROWS
        column = lax.broadcasted_iota(jnp.int32, scores.shape, 1)
        scores = jnp.where(row >= column, scores, -1e30)
        peak = jnp.max(scores, 1, keepdims=True)
        raised = jnp.exp2(scores * factor - peak * factor)
        m_ref[part] = jnp.broadcast_to(peak, (ROWS, HEAD_DIM))
        l_ref[part] = jnp.broadcast_to(jnp.sum(raised, 1, keepdims=True), (ROWS, HEAD_DIM))
        acc_ref[part] = jnp.dot(
            raised.astype(jnp.bfloat16), fresh_v[:reach], preferred_element_type=jnp.float32
        )

    for index, (rank, source) in enumerate(chunks):

        def step(masked, index=index, rank=rank, source=source):
            keys = kv[pl.ds(source, SLOTS), rank, 0].reshape(span, HEAD_DIM)
            values = kv[pl.ds(source, SLOTS), rank, 1].reshape(span, HEAD_DIM)
            for tile in range(tiles):
                part = pl.ds(tile * ROWS, ROWS)
                scores = lax.dot_general(q[part], keys, NT, preferred_element_type=jnp.float32)
                if masked:
                    scores = scores + bias[index : index + 1]
                update(part, scores, values)

        pl.when(state[index] == 2)(functools.partial(step, False))
        pl.when(state[index] == 1)(functools.partial(step, True))

    for tile in range(tiles):
        part = pl.ds(tile * ROWS, ROWS)
        out[part] = (acc_ref[part] / l_ref[part, :1]).astype(out.dtype)


def attend(first, heads, state, bias, query, arrived, fresh_k, fresh_v):
    rows = query.shape[0]
    sources, ranks, _, page_len, _ = arrived.shape
    chunks = [(rank, source) for rank in range(ranks) for source in range(0, sources, SLOTS)]
    own = pl.BlockSpec((rows, HEAD_DIM), lambda h, state: (0, first + h))
    factor = HEAD_DIM ** -0.5 * 1.4426950408889634
    return pl.pallas_call(
        functools.partial(attend_kernel, factor, chunks),
        out_shape=jax.ShapeDtypeStruct((rows, heads * HEAD_DIM), jnp.bfloat16),
        grid_spec=pltpu.PrefetchScalarGridSpec(
            num_scalar_prefetch=1,
            grid=(heads,),
            in_specs=[
                own,
                pl.BlockSpec(
                    (sources, ranks, 2, page_len, HEAD_DIM), lambda h, state: (0, 0, 0, 0, h)
                ),
                own,
                own,
                pl.BlockSpec(bias.shape, lambda h, state: (0, 0)),
            ],
            out_specs=pl.BlockSpec((rows, HEAD_DIM), lambda h, state: (0, h)),
            scratch_shapes=[pltpu.VMEM((rows, HEAD_DIM), jnp.float32) for _ in range(3)],
        ),
        compiler_params=pltpu.CompilerParams(vmem_limit_bytes=48 * 2**20),
        cost_estimate=pl.CostEstimate(
            flops=heads * rows * 5000 * 512, bytes_accessed=heads * 3 * 2**20, transcendentals=0
        ),
        name="attend",
    )(state, query, arrived, fresh_k, fresh_v, bias)


def body(
    tokens,
    q_weight,
    k_weight,
    v_weight,
    o_weight,
    q_gain,
    k_gain,
    post_gain,
    key_pool,
    value_pool,
    cache_len,
    page_table,
):
    req_dev, block_len, feature_part = tokens.shape
    model_width = q_weight.shape[0]
    columns = q_weight.shape[1]
    owners = lax.axis_size("req")
    owner = lax.axis_index("req")
    tensor_size = lax.axis_size("tp")
    flat = tokens.reshape(block_len, feature_part)
    pool_dev, page_len = key_pool.shape[:2]
    pair_cap = pool_dev // owners

    source, rank, valid, local = page_slots(page_table, pool_dev)
    match = (
        valid[:, None, :]
        & (source[:, None, :] == owner)
        & (rank[:, None, :] == jnp.arange(pair_cap)[None, :, None])
    )
    chosen = jnp.sum(jnp.where(match, local[:, None, :], 0), -1).reshape(-1)
    length = lax.dynamic_index_in_dim(cache_len, owner, 0, keepdims=False)
    mine_source = lax.dynamic_index_in_dim(source, owner, 0, keepdims=False)
    mine_rank = lax.dynamic_index_in_dim(rank, owner, 0, keepdims=False)
    mine_valid = lax.dynamic_index_in_dim(valid, owner, 0, keepdims=False)
    held = jnp.clip(length - jnp.arange(page_table.shape[1]) * page_len, 0, page_len)
    place = (
        mine_valid[None, None, :]
        & (mine_rank[None, None, :] == jnp.arange(pair_cap)[:, None, None])
        & (mine_source[None, None, :] == jnp.arange(owners)[None, :, None])
    )
    count = jnp.sum(jnp.where(place, held[None, None, :], 0), -1).reshape(-1, SLOTS)
    state = jnp.where(
        jnp.all(count == page_len, 1), 2, jnp.where(jnp.any(count > 0, 1), 1, 0)
    ).astype(jnp.int32)
    bias = jnp.where(jnp.arange(page_len)[None, None, :] < count[:, :, None], 0.0, -1e30)
    bias = bias.astype(jnp.float32).reshape(count.shape[0], SLOTS * page_len)

    piece = lax.all_gather(flat, "tp", axis=1, tiled=True)

    arrived = []
    first = 0
    groups = head_groups(columns // HEAD_DIM)
    for heads in groups:
        width = heads * HEAD_DIM
        outgoing = collect(first * HEAD_DIM, width, chosen, key_pool, value_pool)
        came = lax.all_to_all(outgoing, "req", split_axis=0, concat_axis=0, tiled=True)
        arrived.append(came.reshape(owners, pair_cap, 2, page_len, width))
        first += heads

    half = o_weight.shape[0] // 2
    mine = lax.dynamic_slice_in_dim(o_weight, (owner % 2) * half, half, 0)
    mine = lax.all_to_all(mine, "tp", split_axis=1, concat_axis=0, tiled=True)
    pairs = [[i, i + 1] for i in range(0, owners, 2)]
    both = lax.all_gather(mine, "req", axis=0, tiled=False, axis_index_groups=pairs)
    o_columns = jnp.transpose(
        both.reshape(2, tensor_size, half, feature_part), (1, 0, 2, 3)
    ).reshape(tensor_size, 2 * half, feature_part)

    q_proj = jnp.dot(piece, q_weight, preferred_element_type=jnp.float32)
    k_proj = jnp.dot(piece, k_weight, preferred_element_type=jnp.float32)
    new_values = jnp.dot(piece, v_weight, preferred_element_type=jnp.float32).astype(jnp.bfloat16)
    q_squares, k_squares = lax.psum(
        (jnp.sum(q_proj * q_proj, 1), jnp.sum(k_proj * k_proj, 1)), "tp"
    )
    full_columns = columns * tensor_size
    q_scale = lax.rsqrt(q_squares / full_columns + EPSILON)[:, None]
    k_scale = lax.rsqrt(k_squares / full_columns + EPSILON)[:, None]
    half_dim = HEAD_DIM // 2
    freqs = jnp.power(
        jnp.float32(ROPE_BASE), -jnp.arange(half_dim, dtype=jnp.float32) * 2.0 / HEAD_DIM
    )
    positions = (length + jnp.arange(block_len, dtype=jnp.int32)).astype(jnp.float32)
    angles = positions[:, None] * freqs
    cos, sin = jnp.cos(angles), jnp.sin(angles)
    query, new_keys = norm_rope(
        q_proj,
        k_proj,
        q_scale,
        k_scale,
        q_gain.astype(jnp.float32)[None],
        k_gain.astype(jnp.float32)[None],
        jnp.concatenate([cos, cos], 1),
        jnp.concatenate([-sin, sin], 1),
    )

    share = None
    first = 0
    for heads, came in zip(groups, arrived):
        attended = attend(first, heads, state, bias, query, came, new_keys, new_values)
        whole = lax.all_gather(attended, "tp", axis=1, tiled=True)
        weight = lax.slice_in_dim(o_columns, first * HEAD_DIM, (first + heads) * HEAD_DIM, axis=1)
        term = jnp.dot(
            whole, weight.reshape(whole.shape[1], feature_part), preferred_element_type=jnp.float32
        )
        share = term if share is None else share + term
        first += heads

    squares = lax.psum(jnp.sum(share * share, 1), "tp")
    normed = share * lax.rsqrt(squares / model_width + EPSILON)[:, None]
    mixed = (flat.astype(jnp.float32) + normed * post_gain.astype(jnp.float32)).astype(jnp.bfloat16)
    return (
        mixed.reshape(req_dev, block_len, feature_part),
        new_keys.reshape(req_dev, block_len, columns),
        new_values.reshape(req_dev, block_len, columns),
    )


def solution(mesh):
    placed = (
        P("req", None, "tp"),
        P(None, "tp"),
        P(None, "tp"),
        P(None, "tp"),
        P("tp", None),
        P("tp"),
        P("tp"),
        P("tp"),
        P("req", None, "tp"),
        P("req", None, "tp"),
        P(),
        P(),
    )
    return jax.shard_map(
        body,
        mesh=mesh,
        in_specs=placed,
        out_specs=(P("req", None, "tp"), P("req", None, "tp"), P("req", None, "tp")),
        check_vma=False,
    )
```

```python
import functools

import jax
import jax.numpy as jnp
from jax import lax
from jax.experimental import pallas as pl
from jax.experimental.pallas import tpu as pltpu
from jax.sharding import PartitionSpec as P

HEAD_DIM = 128
EPSILON = 1e-06
ROPE_BASE = 500000.0
ROWS = 256
SLOTS = 8


def head_groups(heads):
    return (2,) * (heads // 2) + (1,) * (heads % 2)


def page_slots(page_table, pool_dev):
    valid = page_table >= 0
    source = jnp.where(valid, page_table // pool_dev, -1)
    local = jnp.where(valid, page_table % pool_dev, 0)
    order = jnp.arange(page_table.shape[1])
    same = (
        (source[:, :, None] == source[:, None, :])
        & valid[:, None, :]
        & (order[None, :, None] > order[None, None, :])
    )
    rank = jnp.sum(same.astype(jnp.int32), -1)
    return (source, rank, valid, local)


def collect_kernel(first, width, chosen, key_pool, value_pool, out, sem):
    columns = pl.ds(first, width)

    def copies(slot):
        page = chosen[slot]
        return (
            pltpu.make_async_copy(key_pool.at[page, :, columns], out.at[slot, 0], sem),
            pltpu.make_async_copy(value_pool.at[page, :, columns], out.at[slot, 1], sem),
        )

    @pl.loop(0, out.shape[0])
    def _(slot):
        for copy in copies(slot):
            copy.start()

    pltpu.make_async_copy(out, out, sem).wait()


def collect(first, width, chosen, key_pool, value_pool):
    slots = chosen.shape[0]
    page_len = key_pool.shape[1]
    return pl.pallas_call(
        functools.partial(collect_kernel, first, width),
        out_shape=jax.ShapeDtypeStruct((slots, 2, page_len, width), key_pool.dtype),
        in_specs=[
            pl.BlockSpec(memory_space=pltpu.SMEM),
            pl.BlockSpec(memory_space=pl.ANY),
            pl.BlockSpec(memory_space=pl.ANY),
        ],
        out_specs=pl.BlockSpec(memory_space=pltpu.VMEM),
        scratch_shapes=[pltpu.SemaphoreType.DMA],
        compiler_params=pltpu.CompilerParams(vmem_limit_bytes=32 * 2**20),
        name="collect",
    )(chosen, key_pool, value_pool)


def norm_rope_kernel(q, k, q_scale, k_scale, q_gain, k_gain, cosine, sine, q_out, k_out):
    cos, sin = cosine[...], sine[...]
    for values, scale, gain, out in ((q, q_scale, q_gain, q_out), (k, k_scale, k_gain, k_out)):
        for head in range(values.shape[1] // HEAD_DIM):
            part = pl.ds(head * HEAD_DIM, HEAD_DIM)
            x = values[:, part] * scale[...] * gain[:, part]
            out[:, part] = (x * cos + pltpu.roll(x, HEAD_DIM // 2, 1) * sin).astype(out.dtype)


def norm_rope(q, k, q_scale, k_scale, q_gain, k_gain, cosine, sine):
    rows, columns = q.shape
    block = ROWS
    wide = pl.BlockSpec((block, columns), lambda i: (i, 0))
    thin = pl.BlockSpec((block, 1), lambda i: (i, 0))
    flat = pl.BlockSpec((1, columns), lambda i: (0, 0))
    half = pl.BlockSpec((block, HEAD_DIM), lambda i: (i, 0))
    shape = jax.ShapeDtypeStruct((rows, columns), jnp.bfloat16)
    return pl.pallas_call(
        norm_rope_kernel,
        grid=(rows // block,),
        out_shape=(shape, shape),
        in_specs=[wide, wide, thin, thin, flat, flat, half, half],
        out_specs=(wide, wide),
        compiler_params=pltpu.CompilerParams(vmem_limit_bytes=32 * 2**20),
        name="norm_rope",
    )(q, k, q_scale, k_scale, q_gain, k_gain, cosine, sine)


NT = (((1,), (1,)), ((), ()))


def attend_kernel(factor, chunks, state, q, kv, fresh_k, fresh_v, bias, out, m_ref, l_ref, acc_ref):
    rows = q.shape[0]
    tiles = rows // ROWS
    span = SLOTS * kv.shape[3]

    def update(part, scores, values):
        m_old = m_ref[part, :1]
        m_new = jnp.maximum(m_old, jnp.max(scores, 1, keepdims=True))
        alpha = jnp.exp2(m_old * factor - m_new * factor)
        raised = jnp.exp2(scores * factor - m_new * factor)
        total = l_ref[part, :1] * alpha + jnp.sum(raised, 1, keepdims=True)
        acc_ref[part] = acc_ref[part] * alpha + jnp.dot(
            raised.astype(jnp.bfloat16), values, preferred_element_type=jnp.float32
        )
        m_ref[part] = jnp.broadcast_to(m_new, (ROWS, HEAD_DIM))
        l_ref[part] = jnp.broadcast_to(total, (ROWS, HEAD_DIM))

    for tile in range(tiles):
        part = pl.ds(tile * ROWS, ROWS)
        reach = (tile + 1) * ROWS
        scores = lax.dot_general(
            q[part], fresh_k[:reach], NT, preferred_element_type=jnp.float32
        )
        row = lax.broadcasted_iota(jnp.int32, scores.shape, 0) + tile * ROWS
        column = lax.broadcasted_iota(jnp.int32, scores.shape, 1)
        scores = jnp.where(row >= column, scores, -1e30)
        peak = jnp.max(scores, 1, keepdims=True)
        raised = jnp.exp2(scores * factor - peak * factor)
        m_ref[part] = jnp.broadcast_to(peak, (ROWS, HEAD_DIM))
        l_ref[part] = jnp.broadcast_to(jnp.sum(raised, 1, keepdims=True), (ROWS, HEAD_DIM))
        acc_ref[part] = jnp.dot(
            raised.astype(jnp.bfloat16), fresh_v[:reach], preferred_element_type=jnp.float32
        )

    for index, (rank, source) in enumerate(chunks):

        def step(masked, index=index, rank=rank, source=source):
            keys = kv[pl.ds(source, SLOTS), rank, 0].reshape(span, HEAD_DIM)
            values = kv[pl.ds(source, SLOTS), rank, 1].reshape(span, HEAD_DIM)
            for tile in range(tiles):
                part = pl.ds(tile * ROWS, ROWS)
                scores = lax.dot_general(q[part], keys, NT, preferred_element_type=jnp.float32)
                if masked:
                    scores = scores + bias[index : index + 1]
                update(part, scores, values)

        pl.when(state[index] == 2)(functools.partial(step, False))
        pl.when(state[index] == 1)(functools.partial(step, True))

    for tile in range(tiles):
        part = pl.ds(tile * ROWS, ROWS)
        out[part] = (acc_ref[part] / l_ref[part, :1]).astype(out.dtype)


def attend(first, heads, state, bias, query, arrived, fresh_k, fresh_v):
    rows = query.shape[0]
    sources, ranks, _, page_len, _ = arrived.shape
    chunks = [(rank, source) for rank in range(ranks) for source in range(0, sources, SLOTS)]
    own = pl.BlockSpec((rows, HEAD_DIM), lambda h, state: (0, first + h))
    factor = HEAD_DIM ** -0.5 * 1.4426950408889634
    return pl.pallas_call(
        functools.partial(attend_kernel, factor, chunks),
        out_shape=jax.ShapeDtypeStruct((rows, heads * HEAD_DIM), jnp.bfloat16),
        grid_spec=pltpu.PrefetchScalarGridSpec(
            num_scalar_prefetch=1,
            grid=(heads,),
            in_specs=[
                own,
                pl.BlockSpec(
                    (sources, ranks, 2, page_len, HEAD_DIM), lambda h, state: (0, 0, 0, 0, h)
                ),
                own,
                own,
                pl.BlockSpec(bias.shape, lambda h, state: (0, 0)),
            ],
            out_specs=pl.BlockSpec((rows, HEAD_DIM), lambda h, state: (0, h)),
            scratch_shapes=[pltpu.VMEM((rows, HEAD_DIM), jnp.float32) for _ in range(3)],
        ),
        compiler_params=pltpu.CompilerParams(vmem_limit_bytes=48 * 2**20),
        cost_estimate=pl.CostEstimate(
            flops=heads * rows * 5000 * 512, bytes_accessed=heads * 3 * 2**20, transcendentals=0
        ),
        name="attend",
    )(state, query, arrived, fresh_k, fresh_v, bias)


def body(
    tokens,
    q_weight,
    k_weight,
    v_weight,
    o_weight,
    q_gain,
    k_gain,
    post_gain,
    key_pool,
    value_pool,
    cache_len,
    page_table,
):
    req_dev, block_len, feature_part = tokens.shape
    model_width = q_weight.shape[0]
    columns = q_weight.shape[1]
    owners = lax.axis_size("req")
    owner = lax.axis_index("req")
    tensor_size = lax.axis_size("tp")
    flat = tokens.reshape(block_len, feature_part)
    pool_dev, page_len = key_pool.shape[:2]
    pair_cap = pool_dev // owners

    source, rank, valid, local = page_slots(page_table, pool_dev)
    match = (
        valid[:, None, :]
        & (source[:, None, :] == owner)
        & (rank[:, None, :] == jnp.arange(pair_cap)[None, :, None])
    )
    chosen = jnp.sum(jnp.where(match, local[:, None, :], 0), -1).reshape(-1)
    length = lax.dynamic_index_in_dim(cache_len, owner, 0, keepdims=False)
    mine_source = lax.dynamic_index_in_dim(source, owner, 0, keepdims=False)
    mine_rank = lax.dynamic_index_in_dim(rank, owner, 0, keepdims=False)
    mine_valid = lax.dynamic_index_in_dim(valid, owner, 0, keepdims=False)
    held = jnp.clip(length - jnp.arange(page_table.shape[1]) * page_len, 0, page_len)
    place = (
        mine_valid[None, None, :]
        & (mine_rank[None, None, :] == jnp.arange(pair_cap)[:, None, None])
        & (mine_source[None, None, :] == jnp.arange(owners)[None, :, None])
    )
    count = jnp.sum(jnp.where(place, held[None, None, :], 0), -1).reshape(-1, SLOTS)
    state = jnp.where(
        jnp.all(count == page_len, 1), 2, jnp.where(jnp.any(count > 0, 1), 1, 0)
    ).astype(jnp.int32)
    bias = jnp.where(jnp.arange(page_len)[None, None, :] < count[:, :, None], 0.0, -1e30)
    bias = bias.astype(jnp.float32).reshape(count.shape[0], SLOTS * page_len)

    piece = lax.all_gather(flat, "tp", axis=1, tiled=True)

    arrived = []
    first = 0
    groups = head_groups(columns // HEAD_DIM)
    for heads in groups:
        width = heads * HEAD_DIM
        outgoing = collect(first * HEAD_DIM, width, chosen, key_pool, value_pool)
        came = lax.all_to_all(outgoing, "req", split_axis=0, concat_axis=0, tiled=True)
        arrived.append(came.reshape(owners, pair_cap, 2, page_len, width))
        first += heads

    half = o_weight.shape[0] // 2
    place_tp = lax.axis_index("tp")
    mine = lax.dynamic_slice_in_dim(o_weight, (owner % 2) * half, half, 0)

    def block_for(index):
        return lax.dynamic_slice_in_dim(mine, index * feature_part, feature_part, 1)

    gathered = jnp.zeros((tensor_size, half, feature_part), mine.dtype)
    for step in range(tensor_size):
        block = block_for((place_tp + step) % tensor_size)
        if step > 0:
            ring = [(i, (i + step) % tensor_size) for i in range(tensor_size)]
            block = lax.ppermute(block, "tp", ring)
        gathered = lax.dynamic_update_index_in_dim(
            gathered, block, (place_tp - step) % tensor_size, 0
        )
    pairs = [[i, i + 1] for i in range(0, owners, 2)]
    both = lax.all_gather(gathered, "req", axis=0, tiled=False, axis_index_groups=pairs)
    o_columns = jnp.transpose(both, (1, 0, 2, 3)).reshape(
        tensor_size, 2 * half, feature_part
    )

    q_proj = jnp.dot(piece, q_weight, preferred_element_type=jnp.float32)
    k_proj = jnp.dot(piece, k_weight, preferred_element_type=jnp.float32)
    new_values = jnp.dot(piece, v_weight, preferred_element_type=jnp.float32).astype(jnp.bfloat16)
    q_squares, k_squares = lax.psum(
        (jnp.sum(q_proj * q_proj, 1), jnp.sum(k_proj * k_proj, 1)), "tp"
    )
    full_columns = columns * tensor_size
    q_scale = lax.rsqrt(q_squares / full_columns + EPSILON)[:, None]
    k_scale = lax.rsqrt(k_squares / full_columns + EPSILON)[:, None]
    half_dim = HEAD_DIM // 2
    freqs = jnp.power(
        jnp.float32(ROPE_BASE), -jnp.arange(half_dim, dtype=jnp.float32) * 2.0 / HEAD_DIM
    )
    positions = (length + jnp.arange(block_len, dtype=jnp.int32)).astype(jnp.float32)
    angles = positions[:, None] * freqs
    cos, sin = jnp.cos(angles), jnp.sin(angles)
    query, new_keys = norm_rope(
        q_proj,
        k_proj,
        q_scale,
        k_scale,
        q_gain.astype(jnp.float32)[None],
        k_gain.astype(jnp.float32)[None],
        jnp.concatenate([cos, cos], 1),
        jnp.concatenate([-sin, sin], 1),
    )

    share = None
    first = 0
    for heads, came in zip(groups, arrived):
        attended = attend(first, heads, state, bias, query, came, new_keys, new_values)
        whole = lax.all_gather(attended, "tp", axis=1, tiled=True)
        weight = lax.slice_in_dim(o_columns, first * HEAD_DIM, (first + heads) * HEAD_DIM, axis=1)
        term = jnp.dot(
            whole, weight.reshape(whole.shape[1], feature_part), preferred_element_type=jnp.float32
        )
        share = term if share is None else share + term
        first += heads

    squares = lax.psum(jnp.sum(share * share, 1), "tp")
    normed = share * lax.rsqrt(squares / model_width + EPSILON)[:, None]
    mixed = (flat.astype(jnp.float32) + normed * post_gain.astype(jnp.float32)).astype(jnp.bfloat16)
    return (
        mixed.reshape(req_dev, block_len, feature_part),
        new_keys.reshape(req_dev, block_len, columns),
        new_values.reshape(req_dev, block_len, columns),
    )


def solution(mesh):
    placed = (
        P("req", None, "tp"),
        P(None, "tp"),
        P(None, "tp"),
        P(None, "tp"),
        P("tp", None),
        P("tp"),
        P("tp"),
        P("tp"),
        P("req", None, "tp"),
        P("req", None, "tp"),
        P(),
        P(),
    )
    return jax.shard_map(
        body,
        mesh=mesh,
        in_specs=placed,
        out_specs=(P("req", None, "tp"), P("req", None, "tp"), P("req", None, "tp")),
        check_vma=False,
    )
```

```python
import functools

import jax
import jax.numpy as jnp
from jax import lax
from jax.experimental import pallas as pl
from jax.experimental.pallas import tpu as pltpu
from jax.sharding import PartitionSpec as P

HEAD_DIM = 128
EPSILON = 1e-06
ROPE_BASE = 500000.0
ROWS = 256
SLOTS = 8


def head_groups(heads):
    return (2,) * (heads // 2) + (1,) * (heads % 2)


def page_slots(page_table, pool_dev):
    valid = page_table >= 0
    source = jnp.where(valid, page_table // pool_dev, -1)
    local = jnp.where(valid, page_table % pool_dev, 0)
    order = jnp.arange(page_table.shape[1])
    same = (
        (source[:, :, None] == source[:, None, :])
        & valid[:, None, :]
        & (order[None, :, None] > order[None, None, :])
    )
    rank = jnp.sum(same.astype(jnp.int32), -1)
    return (source, rank, valid, local)


def collect_kernel(first, width, chosen, key_pool, value_pool, out, sem):
    columns = pl.ds(first, width)

    def copies(slot):
        page = chosen[slot]
        return (
            pltpu.make_async_copy(key_pool.at[page, :, columns], out.at[slot, 0], sem),
            pltpu.make_async_copy(value_pool.at[page, :, columns], out.at[slot, 1], sem),
        )

    @pl.loop(0, out.shape[0])
    def _(slot):
        for copy in copies(slot):
            copy.start()

    pltpu.make_async_copy(out, out, sem).wait()


def collect(first, width, chosen, key_pool, value_pool):
    slots = chosen.shape[0]
    page_len = key_pool.shape[1]
    return pl.pallas_call(
        functools.partial(collect_kernel, first, width),
        out_shape=jax.ShapeDtypeStruct((slots, 2, page_len, width), key_pool.dtype),
        in_specs=[
            pl.BlockSpec(memory_space=pltpu.SMEM),
            pl.BlockSpec(memory_space=pl.ANY),
            pl.BlockSpec(memory_space=pl.ANY),
        ],
        out_specs=pl.BlockSpec(memory_space=pltpu.VMEM),
        scratch_shapes=[pltpu.SemaphoreType.DMA],
        compiler_params=pltpu.CompilerParams(vmem_limit_bytes=32 * 2**20),
        name="collect",
    )(chosen, key_pool, value_pool)


def norm_rope_kernel(q, k, q_scale, k_scale, q_gain, k_gain, cosine, sine, q_out, k_out):
    cos, sin = cosine[...], sine[...]
    for values, scale, gain, out in ((q, q_scale, q_gain, q_out), (k, k_scale, k_gain, k_out)):
        for head in range(values.shape[1] // HEAD_DIM):
            part = pl.ds(head * HEAD_DIM, HEAD_DIM)
            x = values[:, part] * scale[...] * gain[:, part]
            out[:, part] = (x * cos + pltpu.roll(x, HEAD_DIM // 2, 1) * sin).astype(out.dtype)


def norm_rope(q, k, q_scale, k_scale, q_gain, k_gain, cosine, sine):
    rows, columns = q.shape
    block = ROWS
    wide = pl.BlockSpec((block, columns), lambda i: (i, 0))
    thin = pl.BlockSpec((block, 1), lambda i: (i, 0))
    flat = pl.BlockSpec((1, columns), lambda i: (0, 0))
    half = pl.BlockSpec((block, HEAD_DIM), lambda i: (i, 0))
    shape = jax.ShapeDtypeStruct((rows, columns), jnp.bfloat16)
    return pl.pallas_call(
        norm_rope_kernel,
        grid=(rows // block,),
        out_shape=(shape, shape),
        in_specs=[wide, wide, thin, thin, flat, flat, half, half],
        out_specs=(wide, wide),
        compiler_params=pltpu.CompilerParams(vmem_limit_bytes=32 * 2**20),
        name="norm_rope",
    )(q, k, q_scale, k_scale, q_gain, k_gain, cosine, sine)


NT = (((1,), (1,)), ((), ()))


def attend_kernel(factor, chunks, state, q, kv, fresh_k, fresh_v, bias, out, m_ref, l_ref, acc_ref):
    rows = q.shape[0]
    tiles = rows // ROWS
    span = SLOTS * kv.shape[3]

    def update(part, scores, values):
        m_old = m_ref[part, :1]
        m_new = jnp.maximum(m_old, jnp.max(scores, 1, keepdims=True))
        alpha = jnp.exp2(m_old * factor - m_new * factor)
        raised = jnp.exp2(scores * factor - m_new * factor)
        total = l_ref[part, :1] * alpha + jnp.sum(raised, 1, keepdims=True)
        acc_ref[part] = acc_ref[part] * alpha + jnp.dot(
            raised.astype(jnp.bfloat16), values, preferred_element_type=jnp.float32
        )
        m_ref[part] = jnp.broadcast_to(m_new, (ROWS, HEAD_DIM))
        l_ref[part] = jnp.broadcast_to(total, (ROWS, HEAD_DIM))

    for tile in range(tiles):
        part = pl.ds(tile * ROWS, ROWS)
        reach = (tile + 1) * ROWS
        scores = lax.dot_general(
            q[part], fresh_k[:reach], NT, preferred_element_type=jnp.float32
        )
        row = lax.broadcasted_iota(jnp.int32, scores.shape, 0) + tile * ROWS
        column = lax.broadcasted_iota(jnp.int32, scores.shape, 1)
        scores = jnp.where(row >= column, scores, -1e30)
        peak = jnp.max(scores, 1, keepdims=True)
        raised = jnp.exp2(scores * factor - peak * factor)
        m_ref[part] = jnp.broadcast_to(peak, (ROWS, HEAD_DIM))
        l_ref[part] = jnp.broadcast_to(jnp.sum(raised, 1, keepdims=True), (ROWS, HEAD_DIM))
        acc_ref[part] = jnp.dot(
            raised.astype(jnp.bfloat16), fresh_v[:reach], preferred_element_type=jnp.float32
        )

    for index, (rank, source) in enumerate(chunks):

        def step(masked, index=index, rank=rank, source=source):
            keys = kv[pl.ds(source, SLOTS), rank, 0].reshape(span, HEAD_DIM)
            values = kv[pl.ds(source, SLOTS), rank, 1].reshape(span, HEAD_DIM)
            for tile in range(tiles):
                part = pl.ds(tile * ROWS, ROWS)
                scores = lax.dot_general(q[part], keys, NT, preferred_element_type=jnp.float32)
                if masked:
                    scores = scores + bias[index : index + 1]
                update(part, scores, values)

        pl.when(state[index] == 2)(functools.partial(step, False))
        pl.when(state[index] == 1)(functools.partial(step, True))

    for tile in range(tiles):
        part = pl.ds(tile * ROWS, ROWS)
        out[part] = (acc_ref[part] / l_ref[part, :1]).astype(out.dtype)


def attend(first, heads, state, bias, query, arrived, fresh_k, fresh_v):
    rows = query.shape[0]
    sources, ranks, _, page_len, _ = arrived.shape
    chunks = [(rank, source) for rank in range(ranks) for source in range(0, sources, SLOTS)]
    own = pl.BlockSpec((rows, HEAD_DIM), lambda h, state: (0, first + h))
    factor = HEAD_DIM ** -0.5 * 1.4426950408889634
    return pl.pallas_call(
        functools.partial(attend_kernel, factor, chunks),
        out_shape=jax.ShapeDtypeStruct((rows, heads * HEAD_DIM), jnp.bfloat16),
        grid_spec=pltpu.PrefetchScalarGridSpec(
            num_scalar_prefetch=1,
            grid=(heads,),
            in_specs=[
                own,
                pl.BlockSpec(
                    (sources, ranks, 2, page_len, HEAD_DIM), lambda h, state: (0, 0, 0, 0, h)
                ),
                own,
                own,
                pl.BlockSpec(bias.shape, lambda h, state: (0, 0)),
            ],
            out_specs=pl.BlockSpec((rows, HEAD_DIM), lambda h, state: (0, h)),
            scratch_shapes=[pltpu.VMEM((rows, HEAD_DIM), jnp.float32) for _ in range(3)],
        ),
        compiler_params=pltpu.CompilerParams(vmem_limit_bytes=48 * 2**20),
        cost_estimate=pl.CostEstimate(
            flops=heads * rows * 5000 * 512, bytes_accessed=heads * 3 * 2**20, transcendentals=0
        ),
        name="attend",
    )(state, query, arrived, fresh_k, fresh_v, bias)


def body(
    tokens,
    q_weight,
    k_weight,
    v_weight,
    o_weight,
    q_gain,
    k_gain,
    post_gain,
    key_pool,
    value_pool,
    cache_len,
    page_table,
):
    req_dev, block_len, feature_part = tokens.shape
    model_width = q_weight.shape[0]
    columns = q_weight.shape[1]
    owners = lax.axis_size("req")
    owner = lax.axis_index("req")
    tensor_size = lax.axis_size("tp")
    flat = tokens.reshape(block_len, feature_part)
    pool_dev, page_len = key_pool.shape[:2]
    pair_cap = pool_dev // owners

    source, rank, valid, local = page_slots(page_table, pool_dev)
    match = (
        valid[:, None, :]
        & (source[:, None, :] == owner)
        & (rank[:, None, :] == jnp.arange(pair_cap)[None, :, None])
    )
    chosen = jnp.sum(jnp.where(match, local[:, None, :], 0), -1).reshape(-1)
    length = lax.dynamic_index_in_dim(cache_len, owner, 0, keepdims=False)
    mine_source = lax.dynamic_index_in_dim(source, owner, 0, keepdims=False)
    mine_rank = lax.dynamic_index_in_dim(rank, owner, 0, keepdims=False)
    mine_valid = lax.dynamic_index_in_dim(valid, owner, 0, keepdims=False)
    held = jnp.clip(length - jnp.arange(page_table.shape[1]) * page_len, 0, page_len)
    place = (
        mine_valid[None, None, :]
        & (mine_rank[None, None, :] == jnp.arange(pair_cap)[:, None, None])
        & (mine_source[None, None, :] == jnp.arange(owners)[None, :, None])
    )
    count = jnp.sum(jnp.where(place, held[None, None, :], 0), -1).reshape(-1, SLOTS)
    state = jnp.where(
        jnp.all(count == page_len, 1), 2, jnp.where(jnp.any(count > 0, 1), 1, 0)
    ).astype(jnp.int32)
    bias = jnp.where(jnp.arange(page_len)[None, None, :] < count[:, :, None], 0.0, -1e30)
    bias = bias.astype(jnp.float32).reshape(count.shape[0], SLOTS * page_len)

    piece = lax.all_gather(flat, "tp", axis=1, tiled=True)

    arrived = []
    first = 0
    groups = head_groups(columns // HEAD_DIM)
    for heads in groups:
        width = heads * HEAD_DIM
        outgoing = collect(first * HEAD_DIM, width, chosen, key_pool, value_pool)
        came = lax.all_to_all(outgoing, "req", split_axis=0, concat_axis=0, tiled=True)
        arrived.append(came.reshape(owners, pair_cap, 2, page_len, width))
        first += heads

    q_proj = jnp.dot(piece, q_weight, preferred_element_type=jnp.float32)
    k_proj = jnp.dot(piece, k_weight, preferred_element_type=jnp.float32)
    new_values = jnp.dot(piece, v_weight, preferred_element_type=jnp.float32).astype(jnp.bfloat16)
    q_squares, k_squares = lax.psum(
        (jnp.sum(q_proj * q_proj, 1), jnp.sum(k_proj * k_proj, 1)), "tp"
    )

    late, q_squares, k_squares = lax.optimization_barrier((o_weight, q_squares, k_squares))
    half = late.shape[0] // 2
    place_tp = lax.axis_index("tp")
    mine = lax.dynamic_slice_in_dim(late, (owner % 2) * half, half, 0)
    blocks = []
    for step in range(tensor_size):
        target = (place_tp + step) % tensor_size
        block = lax.dynamic_slice_in_dim(mine, target * feature_part, feature_part, 1)
        if step > 0:
            ring = [(i, (i + step) % tensor_size) for i in range(tensor_size)]
            block = lax.ppermute(block, "tp", ring)
        blocks.append(block)
    pairs = [[i, i + 1] for i in range(0, owners, 2)]
    both = lax.all_gather(
        jnp.stack(blocks), "req", axis=0, tiled=False, axis_index_groups=pairs
    )
    order = (place_tp - jnp.arange(tensor_size)) % tensor_size
    o_columns = jnp.transpose(both, (1, 0, 2, 3))[order].reshape(
        tensor_size, 2 * half, feature_part
    )

    full_columns = columns * tensor_size
    q_scale = lax.rsqrt(q_squares / full_columns + EPSILON)[:, None]
    k_scale = lax.rsqrt(k_squares / full_columns + EPSILON)[:, None]
    half_dim = HEAD_DIM // 2
    freqs = jnp.power(
        jnp.float32(ROPE_BASE), -jnp.arange(half_dim, dtype=jnp.float32) * 2.0 / HEAD_DIM
    )
    positions = (length + jnp.arange(block_len, dtype=jnp.int32)).astype(jnp.float32)
    angles = positions[:, None] * freqs
    cos, sin = jnp.cos(angles), jnp.sin(angles)
    query, new_keys = norm_rope(
        q_proj,
        k_proj,
        q_scale,
        k_scale,
        q_gain.astype(jnp.float32)[None],
        k_gain.astype(jnp.float32)[None],
        jnp.concatenate([cos, cos], 1),
        jnp.concatenate([-sin, sin], 1),
    )

    share = None
    first = 0
    for heads, came in zip(groups, arrived):
        attended = attend(first, heads, state, bias, query, came, new_keys, new_values)
        whole = lax.all_gather(attended, "tp", axis=1, tiled=True)
        weight = lax.slice_in_dim(o_columns, first * HEAD_DIM, (first + heads) * HEAD_DIM, axis=1)
        term = jnp.dot(
            whole, weight.reshape(whole.shape[1], feature_part), preferred_element_type=jnp.float32
        )
        share = term if share is None else share + term
        first += heads

    squares = lax.psum(jnp.sum(share * share, 1), "tp")
    normed = share * lax.rsqrt(squares / model_width + EPSILON)[:, None]
    mixed = (flat.astype(jnp.float32) + normed * post_gain.astype(jnp.float32)).astype(jnp.bfloat16)
    return (
        mixed.reshape(req_dev, block_len, feature_part),
        new_keys.reshape(req_dev, block_len, columns),
        new_values.reshape(req_dev, block_len, columns),
    )


def solution(mesh):
    placed = (
        P("req", None, "tp"),
        P(None, "tp"),
        P(None, "tp"),
        P(None, "tp"),
        P("tp", None),
        P("tp"),
        P("tp"),
        P("tp"),
        P("req", None, "tp"),
        P("req", None, "tp"),
        P(),
        P(),
    )
    return jax.shard_map(
        body,
        mesh=mesh,
        in_specs=placed,
        out_specs=(P("req", None, "tp"), P("req", None, "tp"), P("req", None, "tp")),
        check_vma=False,
    )
```

```python
import functools

import jax
import jax.numpy as jnp
from jax import lax
from jax.experimental import pallas as pl
from jax.experimental.pallas import tpu as pltpu
from jax.sharding import PartitionSpec as P

HEAD_DIM = 128
EPSILON = 1e-06
ROPE_BASE = 500000.0
ROWS = 256
SLOTS = 8


def head_groups(heads):
    return (2,) * (heads // 2) + (1,) * (heads % 2)


def page_slots(page_table, pool_dev):
    valid = page_table >= 0
    source = jnp.where(valid, page_table // pool_dev, -1)
    local = jnp.where(valid, page_table % pool_dev, 0)
    order = jnp.arange(page_table.shape[1])
    same = (
        (source[:, :, None] == source[:, None, :])
        & valid[:, None, :]
        & (order[None, :, None] > order[None, None, :])
    )
    rank = jnp.sum(same.astype(jnp.int32), -1)
    return (source, rank, valid, local)


def collect_kernel(first, width, chosen, key_pool, value_pool, out, sem):
    columns = pl.ds(first, width)

    def copies(slot):
        page = chosen[slot]
        return (
            pltpu.make_async_copy(key_pool.at[page, :, columns], out.at[slot, 0], sem),
            pltpu.make_async_copy(value_pool.at[page, :, columns], out.at[slot, 1], sem),
        )

    @pl.loop(0, out.shape[0])
    def _(slot):
        for copy in copies(slot):
            copy.start()

    pltpu.make_async_copy(out, out, sem).wait()


def collect(first, width, chosen, key_pool, value_pool):
    slots = chosen.shape[0]
    page_len = key_pool.shape[1]
    return pl.pallas_call(
        functools.partial(collect_kernel, first, width),
        out_shape=jax.ShapeDtypeStruct((slots, 2, page_len, width), key_pool.dtype),
        in_specs=[
            pl.BlockSpec(memory_space=pltpu.SMEM),
            pl.BlockSpec(memory_space=pl.ANY),
            pl.BlockSpec(memory_space=pl.ANY),
        ],
        out_specs=pl.BlockSpec(memory_space=pltpu.VMEM),
        scratch_shapes=[pltpu.SemaphoreType.DMA],
        compiler_params=pltpu.CompilerParams(vmem_limit_bytes=32 * 2**20),
        name="collect",
    )(chosen, key_pool, value_pool)


def norm_rope_kernel(q, k, q_scale, k_scale, q_gain, k_gain, cosine, sine, q_out, k_out):
    cos, sin = cosine[...], sine[...]
    for values, scale, gain, out in ((q, q_scale, q_gain, q_out), (k, k_scale, k_gain, k_out)):
        for head in range(values.shape[1] // HEAD_DIM):
            part = pl.ds(head * HEAD_DIM, HEAD_DIM)
            x = values[:, part] * scale[...] * gain[:, part]
            out[:, part] = (x * cos + pltpu.roll(x, HEAD_DIM // 2, 1) * sin).astype(out.dtype)


def norm_rope(q, k, q_scale, k_scale, q_gain, k_gain, cosine, sine):
    rows, columns = q.shape
    block = ROWS
    wide = pl.BlockSpec((block, columns), lambda i: (i, 0))
    thin = pl.BlockSpec((block, 1), lambda i: (i, 0))
    flat = pl.BlockSpec((1, columns), lambda i: (0, 0))
    half = pl.BlockSpec((block, HEAD_DIM), lambda i: (i, 0))
    shape = jax.ShapeDtypeStruct((rows, columns), jnp.bfloat16)
    return pl.pallas_call(
        norm_rope_kernel,
        grid=(rows // block,),
        out_shape=(shape, shape),
        in_specs=[wide, wide, thin, thin, flat, flat, half, half],
        out_specs=(wide, wide),
        compiler_params=pltpu.CompilerParams(vmem_limit_bytes=32 * 2**20),
        name="norm_rope",
    )(q, k, q_scale, k_scale, q_gain, k_gain, cosine, sine)


NT = (((1,), (1,)), ((), ()))


def attend_kernel(factor, chunks, state, q, kv, fresh_k, fresh_v, bias, out, m_ref, l_ref, acc_ref):
    rows = q.shape[0]
    tiles = rows // ROWS
    span = SLOTS * kv.shape[3]

    def update(part, scores, values):
        m_old = m_ref[part, :1]
        m_new = jnp.maximum(m_old, jnp.max(scores, 1, keepdims=True))
        alpha = jnp.exp2(m_old * factor - m_new * factor)
        raised = jnp.exp2(scores * factor - m_new * factor)
        total = l_ref[part, :1] * alpha + jnp.sum(raised, 1, keepdims=True)
        acc_ref[part] = acc_ref[part] * alpha + jnp.dot(
            raised.astype(jnp.bfloat16), values, preferred_element_type=jnp.float32
        )
        m_ref[part] = jnp.broadcast_to(m_new, (ROWS, HEAD_DIM))
        l_ref[part] = jnp.broadcast_to(total, (ROWS, HEAD_DIM))

    for tile in range(tiles):
        part = pl.ds(tile * ROWS, ROWS)
        reach = (tile + 1) * ROWS
        scores = lax.dot_general(
            q[part], fresh_k[:reach], NT, preferred_element_type=jnp.float32
        )
        row = lax.broadcasted_iota(jnp.int32, scores.shape, 0) + tile * ROWS
        column = lax.broadcasted_iota(jnp.int32, scores.shape, 1)
        scores = jnp.where(row >= column, scores, -1e30)
        peak = jnp.max(scores, 1, keepdims=True)
        raised = jnp.exp2(scores * factor - peak * factor)
        m_ref[part] = jnp.broadcast_to(peak, (ROWS, HEAD_DIM))
        l_ref[part] = jnp.broadcast_to(jnp.sum(raised, 1, keepdims=True), (ROWS, HEAD_DIM))
        acc_ref[part] = jnp.dot(
            raised.astype(jnp.bfloat16), fresh_v[:reach], preferred_element_type=jnp.float32
        )

    for index, (rank, source) in enumerate(chunks):

        def step(masked, index=index, rank=rank, source=source):
            keys = kv[pl.ds(source, SLOTS), rank, 0].reshape(span, HEAD_DIM)
            values = kv[pl.ds(source, SLOTS), rank, 1].reshape(span, HEAD_DIM)
            for tile in range(tiles):
                part = pl.ds(tile * ROWS, ROWS)
                scores = lax.dot_general(q[part], keys, NT, preferred_element_type=jnp.float32)
                if masked:
                    scores = scores + bias[index : index + 1]
                update(part, scores, values)

        pl.when(state[index] == 2)(functools.partial(step, False))
        pl.when(state[index] == 1)(functools.partial(step, True))

    for tile in range(tiles):
        part = pl.ds(tile * ROWS, ROWS)
        out[part] = (acc_ref[part] / l_ref[part, :1]).astype(out.dtype)


def attend(first, heads, state, bias, query, arrived, fresh_k, fresh_v):
    rows = query.shape[0]
    sources, ranks, _, page_len, _ = arrived.shape
    chunks = [(rank, source) for rank in range(ranks) for source in range(0, sources, SLOTS)]
    own = pl.BlockSpec((rows, HEAD_DIM), lambda h, state: (0, first + h))
    factor = HEAD_DIM ** -0.5 * 1.4426950408889634
    return pl.pallas_call(
        functools.partial(attend_kernel, factor, chunks),
        out_shape=jax.ShapeDtypeStruct((rows, heads * HEAD_DIM), jnp.bfloat16),
        grid_spec=pltpu.PrefetchScalarGridSpec(
            num_scalar_prefetch=1,
            grid=(heads,),
            in_specs=[
                own,
                pl.BlockSpec(
                    (sources, ranks, 2, page_len, HEAD_DIM), lambda h, state: (0, 0, 0, 0, h)
                ),
                own,
                own,
                pl.BlockSpec(bias.shape, lambda h, state: (0, 0)),
            ],
            out_specs=pl.BlockSpec((rows, HEAD_DIM), lambda h, state: (0, h)),
            scratch_shapes=[pltpu.VMEM((rows, HEAD_DIM), jnp.float32) for _ in range(3)],
        ),
        compiler_params=pltpu.CompilerParams(vmem_limit_bytes=48 * 2**20),
        cost_estimate=pl.CostEstimate(
            flops=heads * rows * 5000 * 512, bytes_accessed=heads * 3 * 2**20, transcendentals=0
        ),
        name="attend",
    )(state, query, arrived, fresh_k, fresh_v, bias)


def body(
    tokens,
    q_weight,
    k_weight,
    v_weight,
    o_weight,
    q_gain,
    k_gain,
    post_gain,
    key_pool,
    value_pool,
    cache_len,
    page_table,
):
    req_dev, block_len, feature_part = tokens.shape
    model_width = q_weight.shape[0]
    columns = q_weight.shape[1]
    owners = lax.axis_size("req")
    owner = lax.axis_index("req")
    tensor_size = lax.axis_size("tp")
    flat = tokens.reshape(block_len, feature_part)
    pool_dev, page_len = key_pool.shape[:2]
    pair_cap = pool_dev // owners

    source, rank, valid, local = page_slots(page_table, pool_dev)
    match = (
        valid[:, None, :]
        & (source[:, None, :] == owner)
        & (rank[:, None, :] == jnp.arange(pair_cap)[None, :, None])
    )
    chosen = jnp.sum(jnp.where(match, local[:, None, :], 0), -1).reshape(-1)
    length = lax.dynamic_index_in_dim(cache_len, owner, 0, keepdims=False)
    mine_source = lax.dynamic_index_in_dim(source, owner, 0, keepdims=False)
    mine_rank = lax.dynamic_index_in_dim(rank, owner, 0, keepdims=False)
    mine_valid = lax.dynamic_index_in_dim(valid, owner, 0, keepdims=False)
    held = jnp.clip(length - jnp.arange(page_table.shape[1]) * page_len, 0, page_len)
    place = (
        mine_valid[None, None, :]
        & (mine_rank[None, None, :] == jnp.arange(pair_cap)[:, None, None])
        & (mine_source[None, None, :] == jnp.arange(owners)[None, :, None])
    )
    count = jnp.sum(jnp.where(place, held[None, None, :], 0), -1).reshape(-1, SLOTS)
    state = jnp.where(
        jnp.all(count == page_len, 1), 2, jnp.where(jnp.any(count > 0, 1), 1, 0)
    ).astype(jnp.int32)
    bias = jnp.where(jnp.arange(page_len)[None, None, :] < count[:, :, None], 0.0, -1e30)
    bias = bias.astype(jnp.float32).reshape(count.shape[0], SLOTS * page_len)

    piece = lax.all_gather(flat, "tp", axis=1, tiled=True)

    arrived = []
    first = 0
    groups = head_groups(columns // HEAD_DIM)
    for heads in groups:
        width = heads * HEAD_DIM
        outgoing = collect(first * HEAD_DIM, width, chosen, key_pool, value_pool)
        if arrived:
            piece, outgoing, arrived[-1] = lax.optimization_barrier((piece, outgoing, arrived[-1]))
        came = lax.all_to_all(outgoing, "req", split_axis=0, concat_axis=0, tiled=True)
        arrived.append(came.reshape(owners, pair_cap, 2, page_len, width))
        first += heads

    q_proj = jnp.dot(piece, q_weight, preferred_element_type=jnp.float32)
    k_proj = jnp.dot(piece, k_weight, preferred_element_type=jnp.float32)
    new_values = jnp.dot(piece, v_weight, preferred_element_type=jnp.float32).astype(jnp.bfloat16)
    q_squares, k_squares = lax.psum(
        (jnp.sum(q_proj * q_proj, 1), jnp.sum(k_proj * k_proj, 1)), "tp"
    )

    late, q_squares, k_squares = lax.optimization_barrier((o_weight, q_squares, k_squares))
    half = late.shape[0] // 2
    place_tp = lax.axis_index("tp")
    mine = lax.dynamic_slice_in_dim(late, (owner % 2) * half, half, 0)
    blocks = []
    for step in range(tensor_size):
        target = (place_tp + step) % tensor_size
        block = lax.dynamic_slice_in_dim(mine, target * feature_part, feature_part, 1)
        if step > 0:
            ring = [(i, (i + step) % tensor_size) for i in range(tensor_size)]
            block = lax.ppermute(block, "tp", ring)
        blocks.append(block)
    pairs = [[i, i + 1] for i in range(0, owners, 2)]
    both = lax.all_gather(
        jnp.stack(blocks), "req", axis=0, tiled=False, axis_index_groups=pairs
    )
    order = (place_tp - jnp.arange(tensor_size)) % tensor_size
    o_columns = jnp.transpose(both, (1, 0, 2, 3))[order].reshape(
        tensor_size, 2 * half, feature_part
    )

    full_columns = columns * tensor_size
    q_scale = lax.rsqrt(q_squares / full_columns + EPSILON)[:, None]
    k_scale = lax.rsqrt(k_squares / full_columns + EPSILON)[:, None]
    half_dim = HEAD_DIM // 2
    freqs = jnp.power(
        jnp.float32(ROPE_BASE), -jnp.arange(half_dim, dtype=jnp.float32) * 2.0 / HEAD_DIM
    )
    positions = (length + jnp.arange(block_len, dtype=jnp.int32)).astype(jnp.float32)
    angles = positions[:, None] * freqs
    cos, sin = jnp.cos(angles), jnp.sin(angles)
    query, new_keys = norm_rope(
        q_proj,
        k_proj,
        q_scale,
        k_scale,
        q_gain.astype(jnp.float32)[None],
        k_gain.astype(jnp.float32)[None],
        jnp.concatenate([cos, cos], 1),
        jnp.concatenate([-sin, sin], 1),
    )

    share = None
    first = 0
    for heads, came in zip(groups, arrived):
        attended = attend(first, heads, state, bias, query, came, new_keys, new_values)
        whole = lax.all_gather(attended, "tp", axis=1, tiled=True)
        weight = lax.slice_in_dim(o_columns, first * HEAD_DIM, (first + heads) * HEAD_DIM, axis=1)
        term = jnp.dot(
            whole, weight.reshape(whole.shape[1], feature_part), preferred_element_type=jnp.float32
        )
        share = term if share is None else share + term
        first += heads

    squares = lax.psum(jnp.sum(share * share, 1), "tp")
    normed = share * lax.rsqrt(squares / model_width + EPSILON)[:, None]
    mixed = (flat.astype(jnp.float32) + normed * post_gain.astype(jnp.float32)).astype(jnp.bfloat16)
    return (
        mixed.reshape(req_dev, block_len, feature_part),
        new_keys.reshape(req_dev, block_len, columns),
        new_values.reshape(req_dev, block_len, columns),
    )


def solution(mesh):
    placed = (
        P("req", None, "tp"),
        P(None, "tp"),
        P(None, "tp"),
        P(None, "tp"),
        P("tp", None),
        P("tp"),
        P("tp"),
        P("tp"),
        P("req", None, "tp"),
        P("req", None, "tp"),
        P(),
        P(),
    )
    return jax.shard_map(
        body,
        mesh=mesh,
        in_specs=placed,
        out_specs=(P("req", None, "tp"), P("req", None, "tp"), P("req", None, "tp")),
        check_vma=False,
    )
```

```python
import functools

import jax
import jax.numpy as jnp
from jax import lax
from jax.experimental import pallas as pl
from jax.experimental.pallas import tpu as pltpu
from jax.sharding import PartitionSpec as P

HEAD_DIM = 128
EPSILON = 1e-06
ROPE_BASE = 500000.0
ROWS = 256
SLOTS = 8


def head_groups(heads):
    return (2,) * (heads // 2) + (1,) * (heads % 2)


def page_slots(page_table, pool_dev):
    valid = page_table >= 0
    source = jnp.where(valid, page_table // pool_dev, -1)
    local = jnp.where(valid, page_table % pool_dev, 0)
    order = jnp.arange(page_table.shape[1])
    same = (
        (source[:, :, None] == source[:, None, :])
        & valid[:, None, :]
        & (order[None, :, None] > order[None, None, :])
    )
    rank = jnp.sum(same.astype(jnp.int32), -1)
    return (source, rank, valid, local)


def collect_kernel(first, width, chosen, key_pool, value_pool, out, sem):
    columns = pl.ds(first, width)

    def copies(slot):
        page = chosen[slot]
        return (
            pltpu.make_async_copy(key_pool.at[page, :, columns], out.at[slot, 0], sem),
            pltpu.make_async_copy(value_pool.at[page, :, columns], out.at[slot, 1], sem),
        )

    @pl.loop(0, out.shape[0])
    def _(slot):
        for copy in copies(slot):
            copy.start()

    pltpu.make_async_copy(out, out, sem).wait()


def collect(first, width, chosen, key_pool, value_pool):
    slots = chosen.shape[0]
    page_len = key_pool.shape[1]
    return pl.pallas_call(
        functools.partial(collect_kernel, first, width),
        out_shape=jax.ShapeDtypeStruct((slots, 2, page_len, width), key_pool.dtype),
        in_specs=[
            pl.BlockSpec(memory_space=pltpu.SMEM),
            pl.BlockSpec(memory_space=pl.ANY),
            pl.BlockSpec(memory_space=pl.ANY),
        ],
        out_specs=pl.BlockSpec(memory_space=pltpu.VMEM),
        scratch_shapes=[pltpu.SemaphoreType.DMA],
        compiler_params=pltpu.CompilerParams(vmem_limit_bytes=32 * 2**20),
        name="collect",
    )(chosen, key_pool, value_pool)


def norm_rope_kernel(q, k, q_scale, k_scale, q_gain, k_gain, cosine, sine, q_out, k_out):
    cos, sin = cosine[...], sine[...]
    for values, scale, gain, out in ((q, q_scale, q_gain, q_out), (k, k_scale, k_gain, k_out)):
        for head in range(values.shape[1] // HEAD_DIM):
            part = pl.ds(head * HEAD_DIM, HEAD_DIM)
            x = values[:, part] * scale[...] * gain[:, part]
            out[:, part] = (x * cos + pltpu.roll(x, HEAD_DIM // 2, 1) * sin).astype(out.dtype)


def norm_rope(q, k, q_scale, k_scale, q_gain, k_gain, cosine, sine):
    rows, columns = q.shape
    block = ROWS
    wide = pl.BlockSpec((block, columns), lambda i: (i, 0))
    thin = pl.BlockSpec((block, 1), lambda i: (i, 0))
    flat = pl.BlockSpec((1, columns), lambda i: (0, 0))
    half = pl.BlockSpec((block, HEAD_DIM), lambda i: (i, 0))
    shape = jax.ShapeDtypeStruct((rows, columns), jnp.bfloat16)
    return pl.pallas_call(
        norm_rope_kernel,
        grid=(rows // block,),
        out_shape=(shape, shape),
        in_specs=[wide, wide, thin, thin, flat, flat, half, half],
        out_specs=(wide, wide),
        compiler_params=pltpu.CompilerParams(vmem_limit_bytes=32 * 2**20),
        name="norm_rope",
    )(q, k, q_scale, k_scale, q_gain, k_gain, cosine, sine)


NT = (((1,), (1,)), ((), ()))


def attend_kernel(factor, chunks, state, q, kv, fresh_k, fresh_v, bias, out, m_ref, l_ref, acc_ref):
    rows = q.shape[0]
    tiles = rows // ROWS
    span = SLOTS * kv.shape[3]

    def update(part, scores, values):
        m_old = m_ref[part, :1]
        m_new = jnp.maximum(m_old, jnp.max(scores, 1, keepdims=True))
        alpha = jnp.exp2(m_old * factor - m_new * factor)
        raised = jnp.exp2(scores * factor - m_new * factor)
        total = l_ref[part, :1] * alpha + jnp.sum(raised, 1, keepdims=True)
        acc_ref[part] = acc_ref[part] * alpha + jnp.dot(
            raised.astype(jnp.bfloat16), values, preferred_element_type=jnp.float32
        )
        m_ref[part] = jnp.broadcast_to(m_new, (ROWS, HEAD_DIM))
        l_ref[part] = jnp.broadcast_to(total, (ROWS, HEAD_DIM))

    for tile in range(tiles):
        part = pl.ds(tile * ROWS, ROWS)
        reach = (tile + 1) * ROWS
        scores = lax.dot_general(
            q[part], fresh_k[:reach], NT, preferred_element_type=jnp.float32
        )
        row = lax.broadcasted_iota(jnp.int32, scores.shape, 0) + tile * ROWS
        column = lax.broadcasted_iota(jnp.int32, scores.shape, 1)
        scores = jnp.where(row >= column, scores, -1e30)
        peak = jnp.max(scores, 1, keepdims=True)
        raised = jnp.exp2(scores * factor - peak * factor)
        m_ref[part] = jnp.broadcast_to(peak, (ROWS, HEAD_DIM))
        l_ref[part] = jnp.broadcast_to(jnp.sum(raised, 1, keepdims=True), (ROWS, HEAD_DIM))
        acc_ref[part] = jnp.dot(
            raised.astype(jnp.bfloat16), fresh_v[:reach], preferred_element_type=jnp.float32
        )

    for index, (rank, source) in enumerate(chunks):

        def step(masked, index=index, rank=rank, source=source):
            keys = kv[pl.ds(source, SLOTS), rank, 0].reshape(span, HEAD_DIM)
            values = kv[pl.ds(source, SLOTS), rank, 1].reshape(span, HEAD_DIM)
            for tile in range(tiles):
                part = pl.ds(tile * ROWS, ROWS)
                scores = lax.dot_general(q[part], keys, NT, preferred_element_type=jnp.float32)
                if masked:
                    scores = scores + bias[index : index + 1]
                update(part, scores, values)

        pl.when(state[index] == 2)(functools.partial(step, False))
        pl.when(state[index] == 1)(functools.partial(step, True))

    for tile in range(tiles):
        part = pl.ds(tile * ROWS, ROWS)
        out[part] = (acc_ref[part] / l_ref[part, :1]).astype(out.dtype)


def attend(first, heads, state, bias, query, arrived, fresh_k, fresh_v):
    rows = query.shape[0]
    sources, ranks, _, page_len, _ = arrived.shape
    chunks = [(rank, source) for rank in range(ranks) for source in range(0, sources, SLOTS)]
    own = pl.BlockSpec((rows, HEAD_DIM), lambda h, state: (0, first + h))
    factor = HEAD_DIM ** -0.5 * 1.4426950408889634
    return pl.pallas_call(
        functools.partial(attend_kernel, factor, chunks),
        out_shape=jax.ShapeDtypeStruct((rows, heads * HEAD_DIM), jnp.bfloat16),
        grid_spec=pltpu.PrefetchScalarGridSpec(
            num_scalar_prefetch=1,
            grid=(heads,),
            in_specs=[
                own,
                pl.BlockSpec(
                    (sources, ranks, 2, page_len, HEAD_DIM), lambda h, state: (0, 0, 0, 0, h)
                ),
                own,
                own,
                pl.BlockSpec(bias.shape, lambda h, state: (0, 0)),
            ],
            out_specs=pl.BlockSpec((rows, HEAD_DIM), lambda h, state: (0, h)),
            scratch_shapes=[pltpu.VMEM((rows, HEAD_DIM), jnp.float32) for _ in range(3)],
        ),
        compiler_params=pltpu.CompilerParams(vmem_limit_bytes=48 * 2**20),
        cost_estimate=pl.CostEstimate(
            flops=heads * rows * 5000 * 512, bytes_accessed=heads * 3 * 2**20, transcendentals=0
        ),
        name="attend",
    )(state, query, arrived, fresh_k, fresh_v, bias)


def body(
    tokens,
    q_weight,
    k_weight,
    v_weight,
    o_weight,
    q_gain,
    k_gain,
    post_gain,
    key_pool,
    value_pool,
    cache_len,
    page_table,
):
    req_dev, block_len, feature_part = tokens.shape
    model_width = q_weight.shape[0]
    columns = q_weight.shape[1]
    owners = lax.axis_size("req")
    owner = lax.axis_index("req")
    tensor_size = lax.axis_size("tp")
    flat = tokens.reshape(block_len, feature_part)
    pool_dev, page_len = key_pool.shape[:2]
    pair_cap = pool_dev // owners

    source, rank, valid, local = page_slots(page_table, pool_dev)
    match = (
        valid[:, None, :]
        & (source[:, None, :] == owner)
        & (rank[:, None, :] == jnp.arange(pair_cap)[None, :, None])
    )
    chosen = jnp.sum(jnp.where(match, local[:, None, :], 0), -1).reshape(-1)
    length = lax.dynamic_index_in_dim(cache_len, owner, 0, keepdims=False)
    mine_source = lax.dynamic_index_in_dim(source, owner, 0, keepdims=False)
    mine_rank = lax.dynamic_index_in_dim(rank, owner, 0, keepdims=False)
    mine_valid = lax.dynamic_index_in_dim(valid, owner, 0, keepdims=False)
    held = jnp.clip(length - jnp.arange(page_table.shape[1]) * page_len, 0, page_len)
    place = (
        mine_valid[None, None, :]
        & (mine_rank[None, None, :] == jnp.arange(pair_cap)[:, None, None])
        & (mine_source[None, None, :] == jnp.arange(owners)[None, :, None])
    )
    count = jnp.sum(jnp.where(place, held[None, None, :], 0), -1).reshape(-1, SLOTS)
    state = jnp.where(
        jnp.all(count == page_len, 1), 2, jnp.where(jnp.any(count > 0, 1), 1, 0)
    ).astype(jnp.int32)
    bias = jnp.where(jnp.arange(page_len)[None, None, :] < count[:, :, None], 0.0, -1e30)
    bias = bias.astype(jnp.float32).reshape(count.shape[0], SLOTS * page_len)

    piece = lax.all_gather(flat, "tp", axis=1, tiled=True)

    arrived = []
    first = 0
    groups = head_groups(columns // HEAD_DIM)
    for heads in groups:
        width = heads * HEAD_DIM
        outgoing = collect(first * HEAD_DIM, width, chosen, key_pool, value_pool)
        if arrived:
            piece, outgoing, arrived[-1] = lax.optimization_barrier((piece, outgoing, arrived[-1]))
        came = lax.all_to_all(outgoing, "req", split_axis=0, concat_axis=0, tiled=True)
        arrived.append(came.reshape(owners, pair_cap, 2, page_len, width))
        first += heads

    q_proj = jnp.dot(piece, q_weight, preferred_element_type=jnp.float32)
    k_proj = jnp.dot(piece, k_weight, preferred_element_type=jnp.float32)
    new_values = jnp.dot(piece, v_weight, preferred_element_type=jnp.float32).astype(jnp.bfloat16)
    q_squares, k_squares = lax.psum(
        (jnp.sum(q_proj * q_proj, 1), jnp.sum(k_proj * k_proj, 1)), "tp"
    )

    late, arrived[-1] = lax.optimization_barrier((o_weight, arrived[-1]))
    half = late.shape[0] // 2
    place_tp = lax.axis_index("tp")
    mine = lax.dynamic_slice_in_dim(late, (owner % 2) * half, half, 0)
    blocks = []
    for step in range(tensor_size):
        target = (place_tp + step) % tensor_size
        block = lax.dynamic_slice_in_dim(mine, target * feature_part, feature_part, 1)
        if step > 0:
            ring = [(i, (i + step) % tensor_size) for i in range(tensor_size)]
            block = lax.ppermute(block, "tp", ring)
        blocks.append(block)
    pairs = [[i, i + 1] for i in range(0, owners, 2)]
    both = lax.all_gather(
        jnp.stack(blocks), "req", axis=0, tiled=False, axis_index_groups=pairs
    )
    order = (place_tp - jnp.arange(tensor_size)) % tensor_size
    o_columns = jnp.transpose(both, (1, 0, 2, 3))[order].reshape(
        tensor_size, 2 * half, feature_part
    )

    full_columns = columns * tensor_size
    q_scale = lax.rsqrt(q_squares / full_columns + EPSILON)[:, None]
    k_scale = lax.rsqrt(k_squares / full_columns + EPSILON)[:, None]
    half_dim = HEAD_DIM // 2
    freqs = jnp.power(
        jnp.float32(ROPE_BASE), -jnp.arange(half_dim, dtype=jnp.float32) * 2.0 / HEAD_DIM
    )
    positions = (length + jnp.arange(block_len, dtype=jnp.int32)).astype(jnp.float32)
    angles = positions[:, None] * freqs
    cos, sin = jnp.cos(angles), jnp.sin(angles)
    query, new_keys = norm_rope(
        q_proj,
        k_proj,
        q_scale,
        k_scale,
        q_gain.astype(jnp.float32)[None],
        k_gain.astype(jnp.float32)[None],
        jnp.concatenate([cos, cos], 1),
        jnp.concatenate([-sin, sin], 1),
    )

    share = None
    first = 0
    for heads, came in zip(groups, arrived):
        attended = attend(first, heads, state, bias, query, came, new_keys, new_values)
        whole = lax.all_gather(attended, "tp", axis=1, tiled=True)
        weight = lax.slice_in_dim(o_columns, first * HEAD_DIM, (first + heads) * HEAD_DIM, axis=1)
        term = jnp.dot(
            whole, weight.reshape(whole.shape[1], feature_part), preferred_element_type=jnp.float32
        )
        share = term if share is None else share + term
        first += heads

    squares = lax.psum(jnp.sum(share * share, 1), "tp")
    normed = share * lax.rsqrt(squares / model_width + EPSILON)[:, None]
    mixed = (flat.astype(jnp.float32) + normed * post_gain.astype(jnp.float32)).astype(jnp.bfloat16)
    return (
        mixed.reshape(req_dev, block_len, feature_part),
        new_keys.reshape(req_dev, block_len, columns),
        new_values.reshape(req_dev, block_len, columns),
    )


def solution(mesh):
    placed = (
        P("req", None, "tp"),
        P(None, "tp"),
        P(None, "tp"),
        P(None, "tp"),
        P("tp", None),
        P("tp"),
        P("tp"),
        P("tp"),
        P("req", None, "tp"),
        P("req", None, "tp"),
        P(),
        P(),
    )
    return jax.shard_map(
        body,
        mesh=mesh,
        in_specs=placed,
        out_specs=(P("req", None, "tp"), P("req", None, "tp"), P("req", None, "tp")),
        check_vma=False,
    )
```
